256 devices in a mesh: grp: 2 (over x_lo), pt: 128 (over x_hi, y, z, core).
Axes of the slice: x: 4 (x_hi: 2, x_lo: 2; x = x_hi * 2 + x_lo), y: 4, z: 8, core: 2. Of those that a mesh axis runs over, the one named last changes fastest.
Arguments:
- left_factor: float32 [16, 128, 2048], P('grp', 'pt'), may hold values from 0 to 7340032, as said below
- right_factor: float32 [128, 128, 2048], P('grp', 'pt'), may hold values from 0 to 7340032, as said below
Outputs:
- product: float32 [16, 128, 4096], P('grp', 'pt')
The draws below stay inside these ranges and needn't reach their ends.
Inputs may be any that keep to these rules, and one draw needn't show every extreme that they name: `left_factor`: every entry is a whole number, a residue modulo 7340033. `right_factor`: every entry is a whole number, a residue modulo 7340033.
All inputs are finite; a program needn't handle non-finite values.
Results may differ from the reference program's by a relative error of at most 0.0003.
Values sent between devices are 32-bit elements; how exact they have to be, the bound alone decides.
A program may use at most 64 MiB of HBM per device.

```python
import jax
import jax.numpy as jnp
import numpy as np
from jax import lax

ORDER = 128
LEFT_ROWS = 16
FIRST = 32
SECOND = 128
COEFFS = 2048


modulus = 7340033


def residues(key, array_shape):
    values = jax.random.randint(key, array_shape, 0, modulus)
    corner = (lax.broadcasted_iota(jnp.int32, array_shape, 0) == 0) & (lax.broadcasted_iota(jnp.int32, array_shape, 1) == 0)
    last_pos = lax.broadcasted_iota(jnp.int32, array_shape, 2)
    values = jnp.where(corner & (last_pos == 0), modulus - 1, values)
    values = jnp.where(corner & (last_pos == 1), 0, values)
    return values.astype(jnp.float32)


def draw_left_factor(key, part):
    return residues(jax.random.fold_in(key, 11), (LEFT_ROWS, ORDER, COEFFS))


def draw_right_factor(key, part):
    return residues(jax.random.fold_in(key, 23), (ORDER, ORDER, COEFFS))


def setup_inputs(seed: int = 0) -> dict:
    seeds = jax.random.split(jax.random.key(seed), 3)
    left_factor = draw_left_factor(jax.random.fold_in(seeds[2], 71), 0)
    right_factor = draw_right_factor(jax.random.fold_in(seeds[2], 71), 0)
    return dict(left_factor=left_factor, right_factor=right_factor)


modulus = 7340033


def root_powers(length_all):
    for generator in range(2, 64):
        candidate = pow(generator, (modulus - 1) // length_all, modulus)
        if pow(candidate, length_all // 2, modulus) == modulus - 1:
            break
    powers = [1]
    for counter in range(length_all - 1):
        powers.append(powers[-1] * candidate % modulus)
    return np.array(powers, dtype=np.int64)


def power_table(powers, exponents):
    return powers[exponents % powers.shape[0]]


def dft_tables():
    length_all = FIRST * SECOND
    powers = root_powers(length_all)
    half_first = np.arange(FIRST // 2)
    range_first = np.arange(FIRST)
    range_second = np.arange(SECOND)
    first_table = power_table(powers, SECOND * np.outer(half_first, range_first))
    twist_table = power_table(powers, np.outer(range_first, range_second))
    second_table = power_table(powers, FIRST * np.outer(range_second, range_second))
    back_first_table = power_table(powers, -FIRST * np.outer(range_second, range_second))
    back_twist_table = power_table(powers, -np.outer(range_second, range_first))
    scale_inv = pow(length_all, modulus - 2, modulus)
    back_second_table = power_table(powers, -SECOND * np.outer(range_first, range_first)) * scale_inv % modulus
    return (first_table, twist_table, second_table, back_first_table, back_twist_table, back_second_table)


def stacked_table(table_np):
    pieces = [(table_np // (256 ** limb_level)) % 256 for limb_level in range(3)]
    stacked = np.zeros((5, 3) + table_np.shape, dtype=np.float32)
    for total_level in range(5):
        for limb_level in range(3):
            partner = total_level - limb_level
            if 0 <= partner < 3:
                stacked[total_level, limb_level] = pieces[partner]
    return stacked


def limb_split(values):
    return [values % 256, (values // 256) % 256, values // 65536]


def fold_sums(level_sums):
    result = level_sums[4] % modulus
    for limb_level in (3, 2, 1, 0):
        result = (result * 256 + level_sums[limb_level]) % modulus
    return result


def times_table(values, table_np):
    left_limbs = limb_split(values)
    right_limbs = limb_split(jnp.asarray(table_np.astype(np.int32)))
    level_sums = []
    for total_level in range(5):
        running = jnp.zeros_like(values)
        for limb_level in range(3):
            partner = total_level - limb_level
            if 0 <= partner < 3:
                running = running + left_limbs[limb_level] * right_limbs[partner]
        level_sums.append(running)
    return fold_sums(level_sums)


def limb_stack(values):
    return jnp.stack([piece.astype(jnp.float32) for piece in limb_split(values)])


def contract(form, values, table_np):
    planes = jnp.einsum(form, limb_stack(values), jnp.asarray(stacked_table(table_np), jnp.float32), precision=lax.Precision.HIGHEST)
    return fold_sums([planes[limb_level].astype(jnp.int32) for limb_level in range(5)])


def forward(rows_in, tables):
    first_table, twist_table, second_table = tables[0], tables[1], tables[2]
    entries = rows_in.shape[0]
    current = rows_in.reshape(entries, FIRST // 2, SECOND)
    current = contract("leab,slac->secb", current, first_table)
    current = times_table(current, twist_table)
    current = contract("lecb,slbd->sdce", current, second_table)
    return current.reshape(FIRST * SECOND, entries)


def inverse(point_values, tables):
    back_first_table, back_twist_table, back_second_table = tables[3], tables[4], tables[5]
    entries = point_values.shape[1]
    current = point_values.reshape(SECOND, FIRST, entries)
    current = contract("ldce,sldb->sebc", current, back_first_table)
    current = times_table(current, back_twist_table)
    current = contract("lebc,slca->seab", current, back_second_table)
    return current.reshape(entries, FIRST * SECOND)


def multiply_points(left_points, right_points):
    planes = jnp.einsum("xpik,ypjk->xypij", limb_stack(left_points), limb_stack(right_points), precision=lax.Precision.HIGHEST)
    level_sums = []
    for total_level in range(5):
        running = jnp.zeros(planes.shape[2:], jnp.int32)
        for limb_level in range(3):
            partner = total_level - limb_level
            if 0 <= partner < 3:
                running = running + planes[limb_level, partner].astype(jnp.int32)
        level_sums.append(running)
    return fold_sums(level_sums)


def reference(left_factor, right_factor):
    tables = dft_tables()

    def evaluate(entry_block):
        return forward(entry_block, tables)

    def to_points(factor):
        blocks = factor.astype(jnp.int32).reshape(-1, ORDER, COEFFS)
        return jnp.moveaxis(lax.map(evaluate, blocks), 0, 1)

    left_points = to_points(left_factor)
    right_points = to_points(right_factor)

    def multiply(pair_in):
        return multiply_points(pair_in[0], pair_in[1])

    products = lax.map(multiply, (left_points.reshape(SECOND, FIRST, LEFT_ROWS, ORDER), right_points.reshape(SECOND, FIRST, ORDER, ORDER)))
    moved = jnp.moveaxis(products.reshape(FIRST * SECOND, LEFT_ROWS, ORDER), 1, 0)

    def interpolate(entry_block):
        return inverse(entry_block, tables)

    coefficients = lax.map(interpolate, moved)
    return coefficients.astype(jnp.float32) / modulus
```

```python
import functools

import jax
import jax.numpy as jnp
import ml_dtypes
import numpy as np
from jax import lax
from jax.experimental import pallas as pl
from jax.experimental.pallas import tpu as pltpu
from jax.sharding import PartitionSpec as P

FIRST = 32
SECOND = 128
LENGTH = FIRST * SECOND
HALF = FIRST // 2
MESH = pl.DeviceIdType.MESH

modulus = 7340033


def root_powers(length_all):
    for generator in range(2, 64):
        candidate = pow(generator, (modulus - 1) // length_all, modulus)
        if pow(candidate, length_all // 2, modulus) == modulus - 1:
            break
    powers = [1]
    for counter in range(length_all - 1):
        powers.append(powers[-1] * candidate % modulus)
    return np.array(powers, dtype=np.int64)


def table_digits(table_np):
    rows = []
    for level in range(3):
        value = table_np * pow(256, level, modulus) % modulus
        value = np.where(value > modulus // 2, value - modulus, value)
        low = (value + 128) % 256 - 128
        rest = (value - low) // 256
        mid = (rest + 128) % 256 - 128
        high = (rest - mid) // 256
        rows.append([piece * 2.0 ** (-8 * level) for piece in (low, mid, high)])
    return np.array(rows).swapaxes(0, 1)


@functools.cache
def tables():
    powers = root_powers(LENGTH)

    def power(exponents):
        return powers[exponents % LENGTH]

    def pack(array):
        return array.astype(np.float32).astype(ml_dtypes.bfloat16)

    a_half, a_all = np.arange(HALF), np.arange(FIRST)
    b_all = np.arange(SECOND)
    eye = np.eye(8)
    first = table_digits(power(SECOND * np.outer(a_all, a_half)))
    first = np.einsum("qlca,ef->qcelfa", first, eye)
    first = first.reshape(3, 8, 4, 8, 3 * 8 * HALF).swapaxes(0, 1).reshape(8, 96, 3 * 8 * HALF)
    expo = FIRST * np.outer(b_all, b_all)[None] + a_all[:, None, None] * b_all[None, None, :]
    second = table_digits(power(expo)).transpose(2, 0, 3, 1, 4).reshape(FIRST, 384, 384)
    third = table_digits(power(-expo)).transpose(2, 1, 3, 0, 4).reshape(FIRST, 384, 384)
    scale = pow(LENGTH, modulus - 2, modulus)
    fourth = table_digits(power(-SECOND * np.outer(a_all, a_all)) * scale % modulus)
    fourth = np.einsum("qlac,ij->qialcj", fourth, eye).reshape(768, 768)
    mask = (np.arange(SECOND)[None, None, :] % 8 == np.arange(8)[:, None, None]) * np.ones((8, 16, 1))
    return tuple(pack(item) for item in (first, second, third, fourth, mask))


def nearest(value):
    return (value + 12582912.0) - 12582912.0


def fold(low, mid, high):
    total = (high * 256.0 + mid) * 256.0 + low
    quotient = nearest(total * (1.0 / modulus))
    rest = mid + 256.0 * (high - 112.0 * quotient)
    return (low - quotient) + 256.0 * rest


def digits(value):
    high = (value + 1.5 * 2.0**39) - 1.5 * 2.0**39
    rest = value - high
    mid = (rest + 1.5 * 2.0**31) - 1.5 * 2.0**31
    return rest - mid, mid, high


def reduce_small(value):
    return value - float(modulus) * nearest(value * (1.0 / modulus))


def times_256(value):
    quotient = nearest(value * (256.0 / modulus))
    return (value * 256.0 - quotient * 7340032.0) - quotient


def narrow(value):
    return value.astype(jnp.bfloat16)


def dot(left, right, transposed=False):
    dims = (((1,), (1 if transposed else 0,)), ((), ()))
    return lax.dot_general(left, right, dims, preferred_element_type=jnp.float32)


def block_transpose(pieces):
    pieces = list(pieces)
    lane = lax.broadcasted_iota(jnp.int32, pieces[0].shape, 1)
    for bit in range(4):
        step, shift = 1 << bit, 8 << bit
        upper = (lane // shift) % 2 == 1
        for index in range(16):
            if index & step:
                continue
            one, two = pieces[index], pieces[index + step]
            pieces[index] = jnp.where(upper, pltpu.roll(two, shift, 1), one)
            pieces[index + step] = jnp.where(upper, two, pltpu.roll(one, SECOND - shift, 1))
    return pieces


CHAIN = ((4, 3), (3, 4))


def kernel(
    right_ref, left_ref, first_ref, second_hbm, third_hbm, fourth_hbm, mask_ref, out_ref,
    xdig, ysend, yrecv, second, third, fourth, ydig, rdig, ldig, pbuf, part, slots, usend, urecv,
    table_sem, send_sem, recv_sem, ring_send, ring_recv, back_send, back_recv,
):
    grp, pt = lax.axis_index("grp"), lax.axis_index("pt")
    core, z = lax.rem(pt, 2), lax.rem(pt // 2, 8)
    my_chunk = (pt // 64) * 4 + lax.rem(pt // 16, 4)
    me = my_chunk * 4 + core * 2 + grp

    def plane(chunk, inner):
        return (inner % 2, (chunk * 8 + z) * 2 + inner // 2)

    def ring(step):
        return (grp, (my_chunk * 8 + lax.rem(z + step + 8, 8)) * 2 + core)

    barrier = pltpu.get_barrier_semaphore()
    for offset in range(8):
        for inner in range(4):
            chunk = lax.rem(my_chunk + offset, 8)

            def greet():
                pl.semaphore_signal(barrier, inc=1, device_id=plane(chunk, inner), device_id_type=MESH)

            if offset == 0:
                pl.when(chunk * 4 + inner != me)(greet)
            else:
                greet()
    for step in (1, -1):
        pl.semaphore_signal(barrier, inc=1, device_id=ring(step), device_id_type=MESH)

    loads = [
        pltpu.make_async_copy(second_hbm.at[me], second, table_sem.at[0]),
        pltpu.make_async_copy(third_hbm.at[me], third, table_sem.at[1]),
        pltpu.make_async_copy(fourth_hbm, fourth, table_sem.at[2]),
    ]
    for load in loads:
        load.start()

    for group in range(9):
        if group < 8:
            block = jnp.concatenate([right_ref[pl.ds(y * 16 + group * 2, 2)] for y in range(4)], axis=0)
        else:
            block = left_ref[...]
        for level, piece in enumerate(digits(block.reshape(128, SECOND))):
            xdig[pl.ds(level * 128, 128), pl.ds(group * SECOND, SECOND)] = narrow(piece)

    pl.semaphore_wait(barrier, 33)

    def first_step(turn, carry):
        chunk = lax.rem(my_chunk + turn, 8)
        sums = dot(first_ref[chunk], xdig[...])
        folded = fold(sums[0:32], sums[32:64], sums[64:96])
        for inner in range(4):
            target = chunk * 4 + inner
            for group in range(9):
                ysend[target, pl.ds(group * 8, 8), :] = folded[
                    inner * 8 : inner * 8 + 8, group * SECOND : (group + 1) * SECOND
                ]

            @pl.when(target != me)
            def _():
                pltpu.make_async_remote_copy(
                    ysend.at[target], yrecv.at[me], send_sem, recv_sem.at[me],
                    device_id=plane(chunk, inner), device_id_type=MESH,
                ).start()

            @pl.when(target == me)
            def _():
                pltpu.make_async_copy(ysend.at[target], yrecv.at[me], recv_sem.at[me]).start()

        return carry

    lax.fori_loop(0, 8, first_step, 0)
    loads[0].wait()

    def second_step(turn, carry):
        chunk = lax.rem(my_chunk + 8 - turn, 8)
        for inner in range(4):
            source = chunk * 4 + inner
            pltpu.make_async_copy(yrecv.at[source], yrecv.at[source], recv_sem.at[source]).wait()
        values = yrecv[pl.ds(chunk * 4, 4), pl.ds(0, 64), :].reshape(256, SECOND)
        for level, piece in enumerate(digits(values)):
            ydig[:, pl.ds(level * SECOND, SECOND)] = narrow(piece)
        sums = dot(second[...], ydig[...], transposed=True)
        folded = fold(sums[0:128], sums[128:256], sums[256:384])
        for level, piece in enumerate(digits(folded)):
            piece = piece.reshape(16, 8, 256)
            both = jnp.concatenate([piece[:, :, :SECOND], piece[:, :, SECOND:]], axis=1)
            rdig[:, level, pl.ds(chunk * 16, 16), :] = narrow(both)
        return carry

    lax.fori_loop(0, 8, second_step, 0)

    values = yrecv[:, pl.ds(64, 8), :].reshape(256, SECOND)
    for level, piece in enumerate(digits(values)):
        ydig[:, pl.ds(level * SECOND, SECOND)] = narrow(piece)
    sums = dot(ydig[...], second[...], transposed=True)
    folded = fold(sums[:, 0:128], sums[:, 128:256], sums[:, 256:384])
    for group, piece in enumerate(block_transpose([folded[k * 16 : k * 16 + 16] for k in range(16)])):
        for level in range(3):
            low, mid, high = digits(piece)
            scale = 2.0 ** (-8 * level)
            ldig[group, 0, level] = narrow(low * scale)
            ldig[group, 1, level] = narrow(mid * (scale / 256.0))
            ldig[group, 2, level] = narrow(high * (scale / 65536.0))
            if level < 2:
                piece = times_256(piece)

    def multiply(group, carry):
        rows = []
        for digit in range(3):
            for d in range(8):
                rows.append(
                    jnp.concatenate([ldig[group, digit, level] * mask_ref[d] for level in range(3)], axis=1)
                )
        sums = dot(jnp.concatenate(rows, axis=0), rdig[group].reshape(384, SECOND))
        pbuf[pl.ds(group * 128, 128), :] = fold(sums[0:128], sums[128:256], sums[256:384])
        return carry

    lax.fori_loop(0, 16, multiply, 0)

    def turn_around(row, carry):
        part[row] = pbuf[pl.ds(row, 128, stride=16), :].T.reshape(2, 8, 8, SECOND)
        return carry

    lax.fori_loop(0, 16, turn_around, 0)

    def hop(half, way, step):
        length = CHAIN[half][way]
        sign = 1 if way == 0 else -1
        block = lax.rem(z + sign * (length - step + 1) + 8, 8)
        slot = (half * 2 + way) * 4 + step - 1
        return block, pltpu.make_async_remote_copy(
            part.at[pl.ds(half * 8, 8), :, block], slots.at[slot], ring_send.at[slot], ring_recv.at[slot],
            device_id=ring(sign), device_id_type=MESH,
        )

    sent = []
    for step in range(1, 5):
        for half in range(2):
            for way in range(2):
                if step > CHAIN[half][way]:
                    continue
                block, copy = hop(half, way, step)
                if step > 1:
                    slot = (half * 2 + way) * 4 + step - 2
                    sent[[item[0] for item in sent].index(slot)][1].wait_recv()
                    part[pl.ds(half * 8, 8), :, block] = part[pl.ds(half * 8, 8), :, block] + slots[slot]
                copy.start()
                sent.append(((half * 2 + way) * 4 + step - 1, copy))

    loads[1].wait()
    for half in range(2):
        total = part[pl.ds(half * 8, 8), :, z]
        for way in range(2):
            slot = (half * 2 + way) * 4 + CHAIN[half][way] - 1
            sent[[item[0] for item in sent].index(slot)][1].wait_recv()
            total = total + reduce_small(slots[slot])
        pieces = [narrow(piece) for piece in digits(total.reshape(128, SECOND))]
        sums = dot(jnp.concatenate(pieces, axis=1), third[...])
        usend[pl.ds(half * 8, 8)] = fold(sums[:, 0:128], sums[:, 128:256], sums[:, 256:384]).reshape(8, 16, SECOND)
        for offset in range(8):
            chunk = lax.rem(my_chunk + offset, 8)
            for core_to in range(2):
                inner = core_to * 2 + half
                row = (chunk // 4) * 8 + lax.rem(chunk, 4) * 2 + core_to
                source = usend.at[pl.ds(half * 8, 8), row]

                def give():
                    pltpu.make_async_remote_copy(
                        source, urecv.at[me], back_send, back_recv, device_id=plane(chunk, inner), device_id_type=MESH
                    ).start()

                def keep():
                    pltpu.make_async_copy(source, urecv.at[me], back_recv).start()

                if offset == 0:
                    pl.when(chunk * 4 + inner != me)(give)
                    pl.when(chunk * 4 + inner == me)(keep)
                else:
                    give()

    loads[2].wait()
    pltpu.make_async_copy(urecv, urecv, back_recv).wait()
    pieces = [narrow(piece) for piece in digits(urecv[...].reshape(256, SECOND))]
    sums = dot(fourth[...], jnp.concatenate(pieces, axis=0))
    folded = fold(sums[0:256], sums[256:512], sums[512:768])
    out_ref[...] = jnp.where(folded < 0, folded + float(modulus), folded)

    pltpu.make_async_copy(ysend.at[pl.ds(0, 31)], ysend.at[pl.ds(0, 31)], send_sem).wait()
    pltpu.make_async_copy(urecv.at[pl.ds(0, 31)], urecv.at[pl.ds(0, 31)], back_send).wait()
    for _, copy in sent:
        copy.wait_send()


def body(left_factor, right_factor):
    first, second, third, fourth, mask = (jnp.asarray(table) for table in tables())
    vmem = pl.BlockSpec(memory_space=pltpu.VMEM)
    hbm = pl.BlockSpec(memory_space=pltpu.HBM)
    f32, bf16 = jnp.float32, jnp.bfloat16
    dma = pltpu.SemaphoreType.DMA
    coefficients = pl.pallas_call(
        kernel,
        out_shape=jax.ShapeDtypeStruct((256, SECOND), f32),
        in_specs=[vmem, vmem, vmem, hbm, hbm, hbm, vmem],
        out_specs=vmem,
        scratch_shapes=[
            pltpu.VMEM((384, 9 * SECOND), bf16),
            pltpu.VMEM((32, 72, SECOND), f32),
            pltpu.VMEM((32, 72, SECOND), f32),
            pltpu.VMEM((384, 384), bf16),
            pltpu.VMEM((384, 384), bf16),
            pltpu.VMEM((768, 768), bf16),
            pltpu.VMEM((256, 384), bf16),
            pltpu.VMEM((16, 3, 128, SECOND), bf16),
            pltpu.VMEM((16, 3, 3, 16, SECOND), bf16),
            pltpu.VMEM((2048, SECOND), f32),
            pltpu.VMEM((16, 2, 8, 8, SECOND), f32),
            pltpu.VMEM((16, 8, 2, 8, SECOND), f32),
            pltpu.VMEM((16, 16, SECOND), f32),
            pltpu.VMEM((32, 8, SECOND), f32),
            dma((3,)),
            dma,
            dma((32,)),
            dma((16,)),
            dma((16,)),
            dma,
            dma,
        ],
        compiler_params=pltpu.CompilerParams(
            collective_id=0, has_side_effects=True, vmem_limit_bytes=48 * 1024 * 1024
        ),
    )(
        right_factor.reshape(64, HALF, SECOND), left_factor.reshape(8, HALF, SECOND),
        first, second, third, fourth, mask,
    )
    return coefficients.reshape(8, 1, LENGTH) / modulus


def solution(mesh):
    return jax.shard_map(
        body,
        mesh=mesh,
        in_specs=(P("grp", "pt", None), P("grp", "pt", None)),
        out_specs=P("grp", "pt", None),
        check_vma=False,
    )
```

```python
import functools

import jax
import jax.numpy as jnp
import ml_dtypes
import numpy as np
from jax import lax
from jax.experimental import pallas as pl
from jax.experimental.pallas import tpu as pltpu
from jax.sharding import PartitionSpec as P

FIRST = 32
SECOND = 128
LENGTH = FIRST * SECOND
HALF = FIRST // 2
MESH = pl.DeviceIdType.MESH

modulus = 7340033


def root_powers(length_all):
    for generator in range(2, 64):
        candidate = pow(generator, (modulus - 1) // length_all, modulus)
        if pow(candidate, length_all // 2, modulus) == modulus - 1:
            break
    powers = [1]
    for counter in range(length_all - 1):
        powers.append(powers[-1] * candidate % modulus)
    return np.array(powers, dtype=np.int64)


def table_digits(table_np):
    rows = []
    for level in range(3):
        value = table_np * pow(256, level, modulus) % modulus
        value = np.where(value > modulus // 2, value - modulus, value)
        low = (value + 128) % 256 - 128
        rest = (value - low) // 256
        mid = (rest + 128) % 256 - 128
        high = (rest - mid) // 256
        rows.append([piece * 2.0 ** (-8 * level) for piece in (low, mid, high)])
    return np.array(rows).swapaxes(0, 1)


@functools.cache
def tables():
    powers = root_powers(LENGTH)

    def power(exponents):
        return powers[exponents % LENGTH]

    def pack(array):
        return array.astype(np.float32).astype(ml_dtypes.bfloat16)

    a_half, a_all = np.arange(HALF), np.arange(FIRST)
    b_all = np.arange(SECOND)
    eye = np.eye(8)
    first = table_digits(power(SECOND * np.outer(a_all, a_half)))
    first = np.einsum("qlca,ef->qcelfa", first, eye)
    first = first.reshape(3, 8, 4, 8, 3 * 8 * HALF).swapaxes(0, 1).reshape(8, 96, 3 * 8 * HALF)
    expo = FIRST * np.outer(b_all, b_all)[None] + a_all[:, None, None] * b_all[None, None, :]
    second = table_digits(power(expo)).transpose(2, 0, 3, 1, 4).reshape(FIRST, 384, 384)
    third = table_digits(power(-expo)).transpose(2, 1, 3, 0, 4).reshape(FIRST, 384, 384)
    scale = pow(LENGTH, modulus - 2, modulus)
    fourth = table_digits(power(-SECOND * np.outer(a_all, a_all)) * scale % modulus)
    fourth = np.einsum("qlac,ij->qialcj", fourth, eye).reshape(768, 768)
    return tuple(pack(item) for item in (first, second, third, fourth))


def nearest(value):
    return (value + 12582912.0) - 12582912.0


def fold(low, mid, high):
    total = (high * 256.0 + mid) * 256.0 + low
    quotient = nearest(total * (1.0 / modulus))
    rest = mid + 256.0 * (high - 112.0 * quotient)
    return (low - quotient) + 256.0 * rest


def digits(value):
    high = (value + 1.5 * 2.0**39) - 1.5 * 2.0**39
    rest = value - high
    mid = (rest + 1.5 * 2.0**31) - 1.5 * 2.0**31
    return rest - mid, mid, high


def reduce_small(value):
    return value - float(modulus) * nearest(value * (1.0 / modulus))


def times_256(value):
    quotient = nearest(value * (256.0 / modulus))
    return (value * 256.0 - quotient * 7340032.0) - quotient


def narrow(value):
    return value.astype(jnp.bfloat16)


def dot(left, right, transposed=False):
    dims = (((1,), (1 if transposed else 0,)), ((), ()))
    return lax.dot_general(left, right, dims, preferred_element_type=jnp.float32)


def block_transpose(pieces):
    pieces = list(pieces)
    lane = lax.broadcasted_iota(jnp.int32, pieces[0].shape, 1)
    for bit in range(4):
        step, shift = 1 << bit, 8 << bit
        upper = (lane // shift) % 2 == 1
        for index in range(16):
            if index & step:
                continue
            one, two = pieces[index], pieces[index + step]
            pieces[index] = jnp.where(upper, pltpu.roll(two, shift, 1), one)
            pieces[index + step] = jnp.where(upper, two, pltpu.roll(one, SECOND - shift, 1))
    return pieces


ORDER = [(dy, dc, dx) for dc in (0, 1) for dy in (2, 1, 3, 0) for dx in (2, 1, 3, 0)]
DELTA = (4, 3, -3, 2, -2, 1, -1, 0)
CHAIN = ((4, 3), (3, 4))


def kernel(
    right_hbm, left_hbm, first_hbm, second_hbm, third_hbm, fourth_hbm, out_ref,
    right_ref, left_ref, first_ref, xdig, send_one, send_two, recv_one, recv_two, second, third, fourth, ydig, rdig, ldig, pbuf, part, slots, usend, urecv,
    table_sem, send_sem, recv_sem, ring_send, ring_recv, back_send, back_recv,
):
    grp, pt = lax.axis_index("grp"), lax.axis_index("pt")
    core, z = lax.rem(pt, 2), lax.rem(pt // 2, 8)
    y, x = lax.rem(pt // 16, 4), (pt // 64) * 2 + grp
    my_chunk = y * 2 + core
    me = my_chunk * 4 + x

    def plane(chunk, inner):
        return (lax.rem(inner, 2), (((inner // 2) * 4 + chunk // 2) * 8 + z) * 2 + lax.rem(chunk, 2))

    def away(dy, dc):
        return lax.rem(y + dy, 4) * 2 + lax.rem(core + dc, 2)

    def ring(step):
        return (grp, (((x // 2) * 4 + y) * 8 + lax.rem(z + step + 8, 8)) * 2 + core)

    loads = [
        pltpu.make_async_copy(source, target, table_sem.at[index])
        for index, (source, target) in enumerate(
            (
                (right_hbm, right_ref), (left_hbm, left_ref), (first_hbm, first_ref),
                (second_hbm.at[me], second), (third_hbm.at[me], third), (fourth_hbm, fourth),
            )
        )
    ]
    for load in loads:
        load.start()

    barrier = pltpu.get_barrier_semaphore()
    for dy, dc, dx in ORDER:
        if (dy, dc, dx) != (0, 0, 0):
            pl.semaphore_signal(
                barrier, inc=1, device_id=plane(away(dy, dc), lax.rem(x + dx, 4)), device_id_type=MESH
            )
    for step in (1, -1):
        pl.semaphore_signal(barrier, inc=1, device_id=ring(step), device_id_type=MESH)

    for load in loads[:3]:
        load.wait()
    for group, delta in enumerate(DELTA[:4] + (None,) + DELTA[4:]):
        if delta is None:
            block = left_ref[...]
        else:
            plane_to = lax.rem(z + delta + 8, 8)
            block = jnp.concatenate([right_ref[pl.ds(row * 16 + plane_to * 2, 2)] for row in range(4)], axis=0)
        for level, piece in enumerate(digits(block.reshape(128, SECOND))):
            xdig[pl.ds(level * 128, 128), pl.ds(group * SECOND, SECOND)] = narrow(piece)

    pl.semaphore_wait(barrier, 33)

    shares = ((send_one, recv_one, 0, 5), (send_two, recv_two, 5, 4))
    for share, (sender, receiver, start, groups) in enumerate(shares):
        for dy, dc, _ in ORDER[::4]:
            chunk = away(dy, dc)
            sums = dot(first_ref[chunk], xdig[:, pl.ds(start * SECOND, groups * SECOND)])
            folded = fold(sums[0:32], sums[32:64], sums[64:96])
            for inner in range(4):
                for group in range(groups):
                    sender[chunk * 4 + inner, pl.ds(group * 8, 8), :] = folded[
                        inner * 8 : inner * 8 + 8, group * SECOND : (group + 1) * SECOND
                    ]
            for dx in (2, 1, 3, 0):
                inner = lax.rem(x + dx, 4)
                target = chunk * 4 + inner
                if (dy, dc, dx) != (0, 0, 0):
                    pltpu.make_async_remote_copy(
                        sender.at[target], receiver.at[me], send_sem.at[share], recv_sem.at[share, me],
                        device_id=plane(chunk, inner), device_id_type=MESH,
                    ).start()
                else:
                    pltpu.make_async_copy(sender.at[target], receiver.at[me], recv_sem.at[share, me]).start()

    loads[3].wait()

    def second_step(share):
        receiver = shares[share][1]
        for pair in range(4):
            chunks = [away(4 - dy, dc) for dy, dc, _ in ORDER[pair * 8 : pair * 8 + 8 : 4]]
            for place, chunk in enumerate(chunks):
                for inner in range(4):
                    source = chunk * 4 + inner
                    pltpu.make_async_copy(
                        receiver.at[source], receiver.at[source], recv_sem.at[share, source]
                    ).wait()
                values = receiver[pl.ds(chunk * 4, 4), pl.ds(0, 32), :].reshape(128, SECOND)
                for level, piece in enumerate(digits(values)):
                    ydig[pl.ds(place * 128, 128), pl.ds(level * SECOND, SECOND)] = narrow(piece)
            sums = dot(second[...], ydig[...], transposed=True)
            folded = fold(sums[0:128], sums[128:256], sums[256:384])
            for place, chunk in enumerate(chunks):
                near = folded[:, place * SECOND : (place + 1) * SECOND]
                both = jnp.concatenate(
                    [near.reshape(16, 8, SECOND), pltpu.roll(near, 64, 1).reshape(16, 8, SECOND)], axis=1
                )
                for level, piece in enumerate(digits(both)):
                    rdig[:, level, pl.ds(chunk * 16, 16), :] = narrow(piece)

    second_step(0)

    values = recv_one[:, pl.ds(32, 8), :].reshape(256, SECOND)
    for level, piece in enumerate(digits(values)):
        ydig[:, pl.ds(level * SECOND, SECOND)] = narrow(piece)
    sums = dot(ydig[...], second[...], transposed=True)
    folded = fold(sums[:, 0:128], sums[:, 128:256], sums[:, 256:384])
    for group, piece in enumerate(block_transpose([folded[k * 16 : k * 16 + 16] for k in range(16)])):
        for level in range(3):
            low, mid, high = digits(piece)
            scale = 2.0 ** (-8 * level)
            for digit, value in enumerate((low * scale, mid * (scale / 256.0), high * (scale / 65536.0))):
                for half in range(2):
                    rows = value[half * 8 : half * 8 + 8]
                    ldig[group, half, digit, level] = narrow(jnp.concatenate([rows, rows], axis=0))
            if level < 2:
                piece = times_256(piece)

    lane = lax.rem(lax.broadcasted_iota(jnp.int32, (16, SECOND), 1), 8)
    upper = lax.broadcasted_iota(jnp.int32, (16, SECOND), 0) // 8
    masks = [narrow(jnp.where(lane == 2 * pair + upper, 1.0, 0.0)) for pair in range(4)]

    def multiply(half):
        def one(group, carry):
            rows = []
            for digit in range(3):
                for d in range(0, 8, 2):
                    pair = [
                        jnp.concatenate([ldig[group, half, digit, level] * masks[d // 2] for level in range(3)], axis=1)
                    ]
                    rows += pair
            sums = dot(jnp.concatenate(rows, axis=0), rdig[group].reshape(384, SECOND))
            pbuf[half, pl.ds(group * 64, 64), :] = fold(sums[0:64], sums[64:128], sums[128:192])
            return carry

        lax.fori_loop(0, 16, one, 0, unroll=4)

    def turn_around(half, share):
        def one(row, carry):
            block = pbuf[half, pl.ds(row, 128, stride=8), :].T[:64].reshape(2, 4, 8, SECOND)
            part[half * 8 + row, :, pl.ds(share * 4, 4)] = block
            return carry

        lax.fori_loop(0, 8, one, 0, unroll=2)

    def hop(half, way, step):
        length = CHAIN[half][way]
        sign = 1 if way == 0 else -1
        delta = sign * (length - step + 1)
        block = DELTA.index(4 if delta == -4 else delta)
        slot = (half * 2 + way) * 4 + step - 1
        return block, pltpu.make_async_remote_copy(
            part.at[pl.ds(half * 8, 8), :, block], slots.at[slot], ring_send.at[slot], ring_recv.at[slot],
            device_id=ring(sign), device_id_type=MESH,
        )

    sent = {}

    def advance(half, step, ways=(0, 1)):
        for way in ways:
            if step > CHAIN[half][way]:
                continue
            block, copy = hop(half, way, step)
            if step > 1:
                sent[half, way, step - 1].wait_recv()
                slot = (half * 2 + way) * 4 + step - 2
                part[pl.ds(half * 8, 8), :, block] = part[pl.ds(half * 8, 8), :, block] + slots[slot]
            copy.start()
            sent[half, way, step] = copy

    multiply(0)
    turn_around(0, 0)
    advance(0, 1)
    multiply(1)
    turn_around(1, 0)
    advance(1, 1)
    second_step(1)
    advance(0, 2, (0,))
    multiply(0)
    turn_around(0, 1)
    advance(0, 2, (1,))
    advance(1, 2)
    multiply(1)
    turn_around(1, 1)
    advance(0, 3)
    advance(1, 3)
    advance(0, 4)
    advance(1, 4)

    loads[4].wait()
    for half in range(2):
        total = part[pl.ds(half * 8, 8), :, DELTA.index(0)]
        for way in range(2):
            slot = (half * 2 + way) * 4 + CHAIN[half][way] - 1
            sent[half, way, CHAIN[half][way]].wait_recv()
            total = total + reduce_small(slots[slot])
        pieces = [narrow(piece) for piece in digits(total.reshape(128, SECOND))]
        sums = dot(jnp.concatenate(pieces, axis=1), third[...])
        usend[pl.ds(half * 8, 8)] = fold(sums[:, 0:128], sums[:, 128:256], sums[:, 256:384]).reshape(8, 16, SECOND)
        for dy, dc, dx in ORDER:
            chunk, inner = away(dy, dc), (x // 2) * 2 + half
            if dx == 0:
                inner = lax.rem(inner, 4)
            elif dx == 2:
                inner = lax.rem(inner + 2, 4)
            else:
                continue
            source = usend.at[pl.ds(half * 8, 8), (inner // 2) * 8 + chunk]

            def give():
                pltpu.make_async_remote_copy(
                    source, urecv.at[me], back_send, back_recv, device_id=plane(chunk, inner), device_id_type=MESH
                ).start()

            def keep():
                pltpu.make_async_copy(source, urecv.at[me], back_recv).start()

            if (dy, dc, dx) == (0, 0, 0):
                pl.when(inner != x)(give)
                pl.when(inner == x)(keep)
            else:
                give()

    loads[5].wait()
    pltpu.make_async_copy(urecv, urecv, back_recv).wait()
    pieces = [narrow(piece) for piece in digits(urecv[...].reshape(256, SECOND))]
    sums = dot(fourth[...], jnp.concatenate(pieces, axis=0))
    folded = fold(sums[0:256], sums[256:512], sums[512:768])
    out_ref[...] = jnp.where(folded < 0, folded + float(modulus), folded)

    for share, (sender, _, _, _) in enumerate(shares):
        pltpu.make_async_copy(sender.at[pl.ds(0, 31)], sender.at[pl.ds(0, 31)], send_sem.at[share]).wait()
    pltpu.make_async_copy(urecv.at[pl.ds(0, 31)], urecv.at[pl.ds(0, 31)], back_send).wait()
    for copy in sent.values():
        copy.wait_send()


def body(left_factor, right_factor):
    first, second, third, fourth = (jnp.asarray(table) for table in tables())
    vmem = pl.BlockSpec(memory_space=pltpu.VMEM)
    hbm = pl.BlockSpec(memory_space=pltpu.HBM)
    f32, bf16 = jnp.float32, jnp.bfloat16
    dma = pltpu.SemaphoreType.DMA
    coefficients = pl.pallas_call(
        kernel,
        out_shape=jax.ShapeDtypeStruct((256, SECOND), f32),
        in_specs=[hbm] * 6,
        out_specs=vmem,
        scratch_shapes=[
            pltpu.VMEM((64, HALF, SECOND), f32),
            pltpu.VMEM((8, HALF, SECOND), f32),
            pltpu.VMEM((8, 96, 384), bf16),
            pltpu.VMEM((384, 9 * SECOND), bf16),
            pltpu.VMEM((32, 40, SECOND), f32),
            pltpu.VMEM((32, 32, SECOND), f32),
            pltpu.VMEM((32, 40, SECOND), f32),
            pltpu.VMEM((32, 32, SECOND), f32),
            pltpu.VMEM((384, 384), bf16),
            pltpu.VMEM((384, 384), bf16),
            pltpu.VMEM((768, 768), bf16),
            pltpu.VMEM((256, 384), bf16),
            pltpu.VMEM((16, 3, 128, SECOND), bf16),
            pltpu.VMEM((16, 2, 3, 3, 16, SECOND), bf16),
            pltpu.VMEM((2, 1024, SECOND), f32),
            pltpu.VMEM((16, 2, 8, 8, SECOND), f32),
            pltpu.VMEM((16, 8, 2, 8, SECOND), f32),
            pltpu.VMEM((16, 16, SECOND), f32),
            pltpu.VMEM((32, 8, SECOND), f32),
            dma((6,)),
            dma((2,)),
            dma((2, 32)),
            dma((16,)),
            dma((16,)),
            dma,
            dma,
        ],
        compiler_params=pltpu.CompilerParams(
            collective_id=0, has_side_effects=True, vmem_limit_bytes=48 * 1024 * 1024
        ),
    )(
        right_factor.reshape(64, HALF, SECOND), left_factor.reshape(8, HALF, SECOND),
        first, second, third, fourth,
    )
    return coefficients.reshape(8, 1, LENGTH) / modulus


def solution(mesh):
    return jax.shard_map(
        body,
        mesh=mesh,
        in_specs=(P("grp", "pt", None), P("grp", "pt", None)),
        out_specs=P("grp", "pt", None),
        check_vma=False,
    )
```

```python
import functools

import jax
import jax.numpy as jnp
import ml_dtypes
import numpy as np
from jax import lax
from jax.experimental import pallas as pl
from jax.experimental.pallas import tpu as pltpu
from jax.sharding import PartitionSpec as P

FIRST = 32
SECOND = 128
LENGTH = FIRST * SECOND
HALF = FIRST // 2
MESH = pl.DeviceIdType.MESH

modulus = 7340033


def root_powers(length_all):
    for generator in range(2, 64):
        candidate = pow(generator, (modulus - 1) // length_all, modulus)
        if pow(candidate, length_all // 2, modulus) == modulus - 1:
            break
    powers = [1]
    for counter in range(length_all - 1):
        powers.append(powers[-1] * candidate % modulus)
    return np.array(powers, dtype=np.int64)


def table_digits(table_np):
    rows = []
    for level in range(3):
        value = table_np * pow(256, level, modulus) % modulus
        value = np.where(value > modulus // 2, value - modulus, value)
        low = (value + 128) % 256 - 128
        rest = (value - low) // 256
        mid = (rest + 128) % 256 - 128
        high = (rest - mid) // 256
        rows.append([piece * 2.0 ** (-8 * level) for piece in (low, mid, high)])
    return np.array(rows).swapaxes(0, 1)


@functools.cache
def tables():
    powers = root_powers(LENGTH)

    def power(exponents):
        return powers[exponents % LENGTH]

    def pack(array):
        return array.astype(np.float32).astype(ml_dtypes.bfloat16)

    a_half, a_all = np.arange(HALF), np.arange(FIRST)
    b_all = np.arange(SECOND)
    eye = np.eye(8)
    first = table_digits(power(SECOND * np.outer(a_all, a_half)))
    first = np.einsum("qlca,ef->qcelfa", first, eye)
    first = first.reshape(3, 8, 4, 8, 3 * 8 * HALF).swapaxes(0, 1).reshape(8, 96, 3 * 8 * HALF)
    expo = FIRST * np.outer(b_all, b_all)[None] + a_all[:, None, None] * b_all[None, None, :]
    second = table_digits(power(expo)).transpose(2, 0, 3, 1, 4).reshape(FIRST, 384, 384)
    third = table_digits(power(-expo)).transpose(2, 1, 3, 0, 4).reshape(FIRST, 384, 384)
    scale = pow(LENGTH, modulus - 2, modulus)
    fourth = table_digits(power(-SECOND * np.outer(a_all, a_all)) * scale % modulus)
    fourth = np.einsum("qlac,ij->qialcj", fourth, eye).reshape(768, 768)
    return tuple(pack(item) for item in (first, second, third, fourth))


def nearest(value):
    return (value + 12582912.0) - 12582912.0


def fold(low, mid, high):
    total = (high * 256.0 + mid) * 256.0 + low
    quotient = nearest(total * (1.0 / modulus))
    rest = mid + 256.0 * (high - 112.0 * quotient)
    return (low - quotient) + 256.0 * rest


def digits(value):
    high = (value + 1.5 * 2.0**39) - 1.5 * 2.0**39
    rest = value - high
    mid = (rest + 1.5 * 2.0**31) - 1.5 * 2.0**31
    return rest - mid, mid, high


def reduce_small(value):
    return value - float(modulus) * nearest(value * (1.0 / modulus))


def times_256(value):
    quotient = nearest(value * (256.0 / modulus))
    return (value * 256.0 - quotient * 7340032.0) - quotient


def narrow(value):
    return value.astype(jnp.bfloat16)


def dot(left, right, transposed=False):
    dims = (((1,), (1 if transposed else 0,)), ((), ()))
    return lax.dot_general(left, right, dims, preferred_element_type=jnp.float32)


def block_transpose(pieces):
    pieces = list(pieces)
    lane = lax.broadcasted_iota(jnp.int32, pieces[0].shape, 1)
    for bit in range(4):
        step, shift = 1 << bit, 8 << bit
        upper = (lane // shift) % 2 == 1
        for index in range(16):
            if index & step:
                continue
            one, two = pieces[index], pieces[index + step]
            pieces[index] = jnp.where(upper, pltpu.roll(two, shift, 1), one)
            pieces[index + step] = jnp.where(upper, two, pltpu.roll(one, SECOND - shift, 1))
    return pieces


ORDER = [(dy, dc, dx) for dc in (0, 1) for dy in (2, 1, 3, 0) for dx in (2, 1, 3, 0)]
DELTA = (4, 3, -3, 2, -2, 1, -1, 0)
SHARES = ((0, 4), (4, 4))
CHAIN = ((4, 3), (3, 4))


def kernel(
    right_hbm, left_hbm, first_hbm, second_hbm, third_hbm, fourth_hbm, out_ref,
    right_ref, left_ref, first_ref, xdig, send_one, send_two, recv_one, recv_two, second, third, fourth, ydig, rdig, ldig, pbuf, part, slots, usend, urecv,
    table_sem, send_sem, recv_sem, ring_send, ring_recv, back_send, back_recv,
):
    grp, pt = lax.axis_index("grp"), lax.axis_index("pt")
    core, z = lax.rem(pt, 2), lax.rem(pt // 2, 8)
    y, x = lax.rem(pt // 16, 4), (pt // 64) * 2 + grp
    my_chunk = y * 2 + core
    me = my_chunk * 4 + x

    def plane(chunk, inner):
        return (lax.rem(inner, 2), (((inner // 2) * 4 + chunk // 2) * 8 + z) * 2 + lax.rem(chunk, 2))

    def away(dy, dc):
        return lax.rem(y + dy, 4) * 2 + lax.rem(core + dc, 2)

    def ring(step):
        return (grp, (((x // 2) * 4 + y) * 8 + lax.rem(z + step + 8, 8)) * 2 + core)

    loads = [
        pltpu.make_async_copy(source, target, table_sem.at[index])
        for index, (source, target) in enumerate(
            (
                (right_hbm, right_ref), (left_hbm, left_ref), (first_hbm, first_ref),
                (second_hbm.at[me], second), (third_hbm.at[me], third), (fourth_hbm, fourth),
            )
        )
    ]
    for load in loads[:3]:
        load.start()

    barrier = pltpu.get_barrier_semaphore()
    for dy, dc, dx in ORDER:
        if (dy, dc, dx) != (0, 0, 0):
            pl.semaphore_signal(
                barrier, inc=1, device_id=plane(away(dy, dc), lax.rem(x + dx, 4)), device_id_type=MESH
            )
    for step in (1, -1):
        pl.semaphore_signal(barrier, inc=1, device_id=ring(step), device_id_type=MESH)

    for load in loads[:3]:
        load.wait()
    for group, delta in enumerate(DELTA[:4] + (None,) + DELTA[4:]):
        if delta is None:
            block = left_ref[...]
        else:
            plane_to = lax.rem(z + delta + 8, 8)
            block = jnp.concatenate([right_ref[pl.ds(row * 16 + plane_to * 2, 2)] for row in range(4)], axis=0)
        for level, piece in enumerate(digits(block.reshape(128, SECOND))):
            xdig[pl.ds(level * 128, 128), pl.ds(group * SECOND, SECOND)] = narrow(piece)

    ydig[...] = jnp.zeros_like(ydig)
    pl.semaphore_wait(barrier, 33)

    shares = ((send_one, recv_one, 0, 5), (send_two, recv_two, 5, 4))
    for share, (sender, receiver, start, groups) in enumerate(shares):
        for dy, dc, _ in ORDER[::4]:
            chunk = away(dy, dc)
            sums = dot(first_ref[chunk], xdig[:, pl.ds(start * SECOND, groups * SECOND)])
            folded = fold(sums[0:32], sums[32:64], sums[64:96])
            for inner in range(4):
                for group in range(groups):
                    sender[chunk * 4 + inner, pl.ds(group * 8, 8), :] = folded[
                        inner * 8 : inner * 8 + 8, group * SECOND : (group + 1) * SECOND
                    ]
            for dx in (2, 1, 3, 0):
                inner = lax.rem(x + dx, 4)
                target = chunk * 4 + inner
                if (dy, dc, dx) != (0, 0, 0):
                    pltpu.make_async_remote_copy(
                        sender.at[target], receiver.at[me], send_sem.at[share], recv_sem.at[share, me],
                        device_id=plane(chunk, inner), device_id_type=MESH,
                    ).start()
                else:
                    pltpu.make_async_copy(sender.at[target], receiver.at[me], recv_sem.at[share, me]).start()
        if share == 0:
            for load in loads[3:]:
                load.start()

    loads[3].wait()

    def second_step(share):
        receiver, rows = shares[share][1], SHARES[share][1] * 8
        for pair in range(4):
            chunks = [away(4 - dy, dc) for dy, dc, _ in ORDER[pair * 8 : pair * 8 + 8 : 4]]
            for place, chunk in enumerate(chunks):
                for inner in range(4):
                    source = chunk * 4 + inner
                    pltpu.make_async_copy(
                        receiver.at[source], receiver.at[source], recv_sem.at[share, source]
                    ).wait()
                values = receiver[pl.ds(chunk * 4, 4), pl.ds(0, rows), :].reshape(4 * rows, SECOND)
                for level, piece in enumerate(digits(values)):
                    ydig[pl.ds(place * 128, 4 * rows), pl.ds(level * SECOND, SECOND)] = narrow(piece)
            sums = dot(second[...], ydig[...], transposed=True)
            folded = fold(sums[0:128], sums[128:256], sums[256:384])
            for place, chunk in enumerate(chunks):
                near = folded[:, place * SECOND : (place + 1) * SECOND]
                both = jnp.concatenate(
                    [near.reshape(16, 8, SECOND), pltpu.roll(near, SECOND - 2 * rows, 1).reshape(16, 8, SECOND)], axis=1
                )
                for level, piece in enumerate(digits(both)):
                    rdig[:, level, pl.ds(chunk * 16, 16), :] = narrow(piece)

    second_step(0)

    values = recv_one[:, pl.ds(32, 8), :].reshape(256, SECOND)
    for level, piece in enumerate(digits(values)):
        ydig[:, pl.ds(level * SECOND, SECOND)] = narrow(piece)
    sums = dot(ydig[...], second[...], transposed=True)
    folded = fold(sums[:, 0:128], sums[:, 128:256], sums[:, 256:384])
    for group, piece in enumerate(block_transpose([folded[k * 16 : k * 16 + 16] for k in range(16)])):
        for level in range(3):
            low, mid, high = digits(piece)
            scale = 2.0 ** (-8 * level)
            for digit, value in enumerate((low * scale, mid * (scale / 256.0), high * (scale / 65536.0))):
                for half in range(2):
                    rows = value[half * 8 : half * 8 + 8]
                    ldig[group, half, digit, level] = narrow(jnp.concatenate([rows, rows], axis=0))
            if level < 2:
                piece = times_256(piece)

    lane = lax.rem(lax.broadcasted_iota(jnp.int32, (16, SECOND), 1), 8)
    upper = lax.broadcasted_iota(jnp.int32, (16, SECOND), 0) // 8
    masks = [narrow(jnp.where(lane == 2 * pair + upper, 1.0, 0.0)) for pair in range(4)]

    def multiply(half):
        def one(group, carry):
            rows = []
            for digit in range(3):
                for d in range(0, 8, 2):
                    pair = [
                        jnp.concatenate([ldig[group, half, digit, level] * masks[d // 2] for level in range(3)], axis=1)
                    ]
                    rows += pair
            sums = dot(jnp.concatenate(rows, axis=0), rdig[group].reshape(384, SECOND))
            pbuf[half, pl.ds(group * 64, 64), :] = fold(sums[0:64], sums[64:128], sums[128:192])
            return carry

        lax.fori_loop(0, 16, one, 0, unroll=8)

    def turn_around(half, share):
        start, count = SHARES[share]

        def one(row, carry):
            turned = pbuf[half, pl.ds(row, 128, stride=8), :].T[: count * 16]
            part[half * 8 + row, :, pl.ds(start, count)] = turned.reshape(2, count, 8, SECOND)
            return carry

        lax.fori_loop(0, 8, one, 0, unroll=2)

    def hop(half, way, step):
        length = CHAIN[half][way]
        sign = 1 if way == 0 else -1
        delta = sign * (length - step + 1)
        block = DELTA.index(4 if delta == -4 else delta)
        slot = (half * 2 + way) * 4 + step - 1
        return block, pltpu.make_async_remote_copy(
            part.at[pl.ds(half * 8, 8), :, block], slots.at[slot], ring_send.at[slot], ring_recv.at[slot],
            device_id=ring(sign), device_id_type=MESH,
        )

    sent = {}

    def advance(half, step, ways=(0, 1)):
        for way in ways:
            if step > CHAIN[half][way]:
                continue
            block, copy = hop(half, way, step)
            if step > 1:
                sent[half, way, step - 1].wait_recv()
                slot = (half * 2 + way) * 4 + step - 2
                part[pl.ds(half * 8, 8), :, block] = part[pl.ds(half * 8, 8), :, block] + slots[slot]
            copy.start()
            sent[half, way, step] = copy

    multiply(0)
    turn_around(0, 0)
    advance(0, 1)
    multiply(1)
    turn_around(1, 0)
    advance(1, 1)
    second_step(1)
    advance(0, 2, (0,))
    multiply(0)
    turn_around(0, 1)
    advance(0, 2, (1,))
    advance(1, 2)
    multiply(1)
    turn_around(1, 1)
    advance(0, 3)
    advance(1, 3)
    advance(0, 4)
    advance(1, 4)

    loads[4].wait()
    for half in range(2):
        total = part[pl.ds(half * 8, 8), :, DELTA.index(0)]
        for way in range(2):
            slot = (half * 2 + way) * 4 + CHAIN[half][way] - 1
            sent[half, way, CHAIN[half][way]].wait_recv()
            total = total + reduce_small(slots[slot])
        pieces = [narrow(piece) for piece in digits(total.reshape(128, SECOND))]
        sums = dot(jnp.concatenate(pieces, axis=1), third[...])
        usend[pl.ds(half * 8, 8)] = fold(sums[:, 0:128], sums[:, 128:256], sums[:, 256:384]).reshape(8, 16, SECOND)
        for dy, dc, dx in ORDER:
            chunk, inner = away(dy, dc), (x // 2) * 2 + half
            if dx == 0:
                inner = lax.rem(inner, 4)
            elif dx == 2:
                inner = lax.rem(inner + 2, 4)
            else:
                continue
            source = usend.at[pl.ds(half * 8, 8), (inner // 2) * 8 + chunk]

            def give():
                pltpu.make_async_remote_copy(
                    source, urecv.at[me], back_send, back_recv, device_id=plane(chunk, inner), device_id_type=MESH
                ).start()

            def keep():
                pltpu.make_async_copy(source, urecv.at[me], back_recv).start()

            if (dy, dc, dx) == (0, 0, 0):
                pl.when(inner != x)(give)
                pl.when(inner == x)(keep)
            else:
                give()

    loads[5].wait()
    pltpu.make_async_copy(urecv, urecv, back_recv).wait()
    pieces = [narrow(piece) for piece in digits(urecv[...].reshape(256, SECOND))]
    sums = dot(fourth[...], jnp.concatenate(pieces, axis=0))
    folded = fold(sums[0:256], sums[256:512], sums[512:768])
    out_ref[...] = jnp.where(folded < 0, folded + float(modulus), folded)

    for share, (sender, _, _, _) in enumerate(shares):
        pltpu.make_async_copy(sender.at[pl.ds(0, 31)], sender.at[pl.ds(0, 31)], send_sem.at[share]).wait()
    pltpu.make_async_copy(urecv.at[pl.ds(0, 31)], urecv.at[pl.ds(0, 31)], back_send).wait()
    for copy in sent.values():
        copy.wait_send()


def body(left_factor, right_factor):
    first, second, third, fourth = (jnp.asarray(table) for table in tables())
    vmem = pl.BlockSpec(memory_space=pltpu.VMEM)
    hbm = pl.BlockSpec(memory_space=pltpu.HBM)
    f32, bf16 = jnp.float32, jnp.bfloat16
    dma = pltpu.SemaphoreType.DMA
    coefficients = pl.pallas_call(
        kernel,
        out_shape=jax.ShapeDtypeStruct((256, SECOND), f32),
        in_specs=[hbm] * 6,
        out_specs=vmem,
        scratch_shapes=[
            pltpu.VMEM((64, HALF, SECOND), f32),
            pltpu.VMEM((8, HALF, SECOND), f32),
            pltpu.VMEM((8, 96, 384), bf16),
            pltpu.VMEM((384, 9 * SECOND), bf16),
            *[pltpu.VMEM((32, rows, SECOND), f32) for rows in (40, 32, 40, 32)],
            pltpu.VMEM((384, 384), bf16),
            pltpu.VMEM((384, 384), bf16),
            pltpu.VMEM((768, 768), bf16),
            pltpu.VMEM((256, 384), bf16),
            pltpu.VMEM((16, 3, 128, SECOND), bf16),
            pltpu.VMEM((16, 2, 3, 3, 16, SECOND), bf16),
            pltpu.VMEM((2, 1024, SECOND), f32),
            pltpu.VMEM((16, 2, 8, 8, SECOND), f32),
            pltpu.VMEM((16, 8, 2, 8, SECOND), f32),
            pltpu.VMEM((16, 16, SECOND), f32),
            pltpu.VMEM((32, 8, SECOND), f32),
            dma((6,)),
            dma((2,)),
            dma((2, 32)),
            dma((16,)),
            dma((16,)),
            dma,
            dma,
        ],
        compiler_params=pltpu.CompilerParams(
            collective_id=0, has_side_effects=True, vmem_limit_bytes=60 * 1024 * 1024
        ),
    )(
        right_factor.reshape(64, HALF, SECOND), left_factor.reshape(8, HALF, SECOND),
        first, second, third, fourth,
    )
    return coefficients.reshape(8, 1, LENGTH) / modulus


def solution(mesh):
    return jax.shard_map(
        body,
        mesh=mesh,
        in_specs=(P("grp", "pt", None), P("grp", "pt", None)),
        out_specs=P("grp", "pt", None),
        check_vma=False,
    )
```
